128 devices in a mesh: tm: 8 (over y, core), rows: 16 (over z, x).
Axes of the slice: x: 4, y: 4, z: 4, core: 2. Of those that a mesh axis runs over, the one named last changes fastest.
Arguments:
- video: bfloat16 [32, 128, 256, 128], P('tm', 'rows'), may hold values from -15 to 15
- clip_lengths: int32 [8], replicated, may hold values from 1 to 9, 32 in all
- norm_gain: float32 [128], replicated, may hold values from 0.5 to 1.5
- norm_shift: float32 [128], replicated, may hold values from -3 to 3
- conv_weight: bfloat16 [3, 3, 3, 128, 128], replicated, may hold values from -0.109375 to 0.109375
- conv_bias: float32 [128], replicated, may hold values from -3 to 3
- down_weight: bfloat16 [3, 3, 3, 128, 128], replicated, may hold values from -0.109375 to 0.109375
- down_bias: float32 [128], replicated, may hold values from -3 to 3
Outputs:
- encoded: bfloat16 [32, 64, 128, 128], P('tm', 'rows')
The draws below stay inside these ranges and needn't reach their ends.
Inputs may be any that keep to these rules, and one draw needn't show every extreme that they name: `clip_lengths`: the lengths sum to 32; the longest clip has exactly 9 frames.
All inputs are finite; a program needn't handle non-finite values.
Results may differ from the reference program's by a relative error of at most 0.0051.
Values may be sent and summed in bfloat16 or wider, within the bound.
A program may use at most 192 MiB of HBM per device.

```python
import math
import jax
import jax.numpy as jnp
import numpy as np
from jax import lax

C = 128
GROUPS = 32
W = 256
FRAMES = 32
H = 128
CLIPS = 8
MOST = 9


def draw_video(key, part):
    key = jax.random.fold_in(key, 11)
    noise_key, local_key, chan_key = jax.random.split(key, 3)
    shape = (FRAMES, H, W, C)
    frame_rise = 3.0 ** (jnp.arange(FRAMES, dtype=jnp.float32) / max(FRAMES - 1, 1))
    row_rise = 3.0 ** (jnp.arange(H, dtype=jnp.float32) / max(H - 1, 1))
    local_scale = jnp.exp(jax.random.uniform(local_key, (FRAMES, H, 1, 1), minval=0.0, maxval=math.log(4.0)))
    chan_scale = jnp.exp(jax.random.uniform(chan_key, (1, 1, 1, C), minval=0.0, maxval=math.log(2.0)))
    scale = 0.05 * frame_rise[:, None, None, None] * row_rise[None, :, None, None] * local_scale * chan_scale
    noise = jax.random.truncated_normal(noise_key, -4.0, 4.0, shape)
    return (scale * noise).astype(jnp.bfloat16)


def split_up(number_of, total, reach, lean):
    loads = [(1 << 20) // math.isqrt(grade ** lean) + 1 for grade in range(2, number_of + 1)]
    surplus, given = total - reach - (number_of - 1), [1] * (number_of - 1)
    while surplus > 0:
        free = [i for i in range(number_of - 1) if given[i] < reach]
        mass, budget = sum([loads[i] for i in free]), surplus
        for i in free:
            addition = min(reach - given[i], max(1, budget * loads[i] // mass), surplus)
            given[i] = given[i] + addition
            surplus = surplus - addition
    return np.array([reach] + given)


def ragged(key, number_of, total, bound, skew):
    if number_of == 2:
        one = jax.random.randint(key, (), max(1, total - bound), min(bound, total - 1) + 1)
        return jnp.stack([one, total - one])
    tallies = jnp.asarray(split_up(number_of, total, bound, skew), jnp.int32)
    couples = (number_of - 1) // 2
    giver, taker = tallies[1:1 + 2 * couples:2], tallies[2:2 + 2 * couples:2]
    margin = jnp.minimum(giver - 1, bound - taker)
    moved = jax.random.randint(jax.random.fold_in(key, 1), (couples,), 0, 1 << 20) % (margin + 1)
    tallies = tallies.at[1:1 + 2 * couples:2].set(giver - moved).at[2:2 + 2 * couples:2].set(taker + moved)
    return tallies[jax.random.permutation(jax.random.fold_in(key, 2), number_of)]


def gaussian(rng, shape, width, bound, kind=jnp.bfloat16):
    return jnp.clip(width * jax.random.normal(rng, shape, jnp.float32), -bound, bound).astype(kind)


def setup_inputs(seed: int = 0) -> dict:
    seeds = jax.random.split(jax.random.key(seed), 9)
    return {
        "video": draw_video(jax.random.fold_in(seeds[8], 71), 0),
        "clip_lengths": ragged(seeds[1], CLIPS, FRAMES, MOST, 1).astype(jnp.int32),
        "norm_gain": jnp.clip(jax.random.uniform(seeds[2], (C,), jnp.float32, 0.5, 1.5), 0.5, 1.5),
        "norm_shift": gaussian(seeds[3], (C,), 0.5, 3.0, jnp.float32),
        "conv_weight": gaussian(seeds[4], (3, 3, 3, C, C), (27 * C) ** -0.5, 0.109375),
        "conv_bias": gaussian(seeds[5], (C,), 0.5, 3.0, jnp.float32),
        "down_weight": gaussian(seeds[6], (3, 3, 3, C, C), (27 * C) ** -0.5, 0.109375),
        "down_bias": gaussian(seeds[7], (C,), 0.5, 3.0, jnp.float32),
    }


EPSILON = 1e-06

def clip_member(clip_lengths, frame_ids):
    clip_ends = jnp.cumsum(clip_lengths, dtype=jnp.int32)
    clip_starts = clip_ends - clip_lengths
    inside = (frame_ids[:, None] >= clip_starts[None, :]) & (frame_ids[:, None] < clip_ends[None, :])
    return inside.astype(jnp.float32)

def clip_first_frame(clip_lengths, frame_ids):
    clip_ends = jnp.cumsum(clip_lengths, dtype=jnp.int32)
    clip_starts = clip_ends - clip_lengths
    inside = (frame_ids[:, None] >= clip_starts[None, :]) & (frame_ids[:, None] < clip_ends[None, :])
    return lax.optimization_barrier(jnp.sum(jnp.where(inside, clip_starts[None, :], 0), axis=1)).astype(jnp.int32)

def reference(video, clip_lengths, norm_gain, norm_shift, conv_weight, conv_bias, down_weight, down_bias):
    per_group = C // GROUPS
    frame_ids = jnp.arange(FRAMES, dtype=jnp.int32)
    member = clip_member(clip_lengths, frame_ids)
    clip_first = clip_first_frame(clip_lengths, frame_ids)

    def moments(frame_block):
        values = frame_block.astype(jnp.float32).reshape(H * W, GROUPS, per_group)
        return (lax.optimization_barrier(jnp.sum(values, axis=(0, 2))), lax.optimization_barrier(jnp.sum(values * values, axis=(0, 2))))
    totals, squares = lax.map(moments, video)
    clip_sum = jnp.dot(member.T, totals, precision=lax.Precision.HIGHEST)
    clip_square = jnp.dot(member.T, squares, precision=lax.Precision.HIGHEST)
    counts = (clip_lengths * (H * W * per_group)).astype(jnp.float32)[:, None]
    means = clip_sum / counts
    scales = lax.rsqrt(clip_square / counts - means * means + EPSILON)
    frame_mean = jnp.repeat(jnp.dot(member, means, precision=lax.Precision.HIGHEST), per_group, axis=1)
    frame_scale = jnp.repeat(jnp.dot(member, scales, precision=lax.Precision.HIGHEST), per_group, axis=1)

    def activate(items):
        frame_block, mean_row, scale_row = items
        normed = (frame_block.astype(jnp.float32) - mean_row) * scale_row * norm_gain + norm_shift
        return jax.nn.silu(normed).astype(jnp.bfloat16)
    hidden = lax.map(activate, (video, frame_mean, frame_scale))
    time_lags = jnp.arange(3, dtype=jnp.int32)
    sources = jnp.maximum(frame_ids[:, None] - 2 + time_lags[None, :], clip_first[:, None])

    def convolve(items):
        frame_index, picks = items
        padded = jnp.pad(hidden[picks], ((0, 0), (1, 1), (1, 1), (0, 0)), mode='edge')
        running = jnp.zeros((H * W, C), jnp.float32)
        for time_tap in range(3):
            for row_tap in range(3):
                for col_tap in range(3):
                    sliced = padded[time_tap, row_tap:row_tap + H, col_tap:col_tap + W].reshape(H * W, C)
                    running = running + jnp.dot(sliced, conv_weight[time_tap, row_tap, col_tap], preferred_element_type=jnp.float32)
        running = running.reshape(H, W, C) + conv_bias + video[frame_index].astype(jnp.float32)
        return running.astype(jnp.bfloat16)
    summed = lax.map(convolve, (frame_ids, sources))

    def reduce_frame(picks):
        padded = jnp.pad(summed[picks], ((0, 0), (1, 0), (1, 0), (0, 0)), mode='edge')
        running = jnp.zeros((H // 2 * (W // 2), C), jnp.float32)
        for time_tap in range(3):
            for row_tap in range(3):
                for col_tap in range(3):
                    sliced = padded[time_tap, row_tap:row_tap + H - 1:2, col_tap:col_tap + W - 1:2]
                    sliced = sliced.reshape(H // 2 * (W // 2), C)
                    running = running + jnp.dot(sliced, down_weight[time_tap, row_tap, col_tap], preferred_element_type=jnp.float32)
        running = running.reshape(H // 2, W // 2, C) + down_bias
        return running.astype(jnp.bfloat16)
    return lax.map(reduce_frame, sources)
```

```python
import jax
import jax.numpy as jnp
from jax import lax
from jax.experimental import pallas as pl
from jax.experimental.pallas import tpu as pltpu
from jax.sharding import PartitionSpec as P

GROUPS = 32
EPSILON = 1e-06
TM, ROWS = 8, 16
FRAMES, BAND, COLS, CH = 4, 8, 256, 128
HEIGHT = BAND * ROWS
PER_GROUP = CH // GROUPS
EXT = FRAMES + 2
OUT_ROWS, OUT_COLS = BAND // 2, COLS // 2
F32, BF16 = jnp.float32, jnp.bfloat16


def kernel(
    video, clip, gain, shift, cw_hbm, cbias, dw_hbm, dbias, out,
    raw, hid, cw, dw, wc, wd, part, tot, rbuf, tbuf, mom, coef, hs, ss, dn,
    rowsend, rowrecv, z, psend, precv,
    load_sem, halo_send, halo_recv, r_send, r_recv, t_send, t_recv,
    row_send, row_recv, p_send, p_recv,
):
    d = lax.axis_index("tm")
    r = lax.axis_index("rows")

    def tm(k):
        return lax.rem(d + (k + TM), TM)

    def rw(k):
        return lax.rem(r + (k + ROWS), ROWS)

    def remote(src, dst, send, recv, k, j):
        return pltpu.make_async_remote_copy(
            src_ref=src, dst_ref=dst, send_sem=send, recv_sem=recv,
            device_id=(tm(k), rw(j)), device_id_type=pl.DeviceIdType.MESH,
        )

    loads = [
        pltpu.make_async_copy(video.at[f], raw.at[2 + f, pl.ds(1, BAND)], load_sem.at[f])
        for f in range(FRAMES)
    ]
    loads.append(pltpu.make_async_copy(cw_hbm, cw, load_sem.at[FRAMES]))
    loads.append(pltpu.make_async_copy(dw_hbm, dw, load_sem.at[FRAMES + 1]))
    for copy in loads:
        copy.start()

    barrier = pltpu.get_barrier_semaphore()
    peers = [(0, j) for j in range(1, ROWS)] + [(k, 0) for k in (-2, -1, 1, 2)]
    peers += [(1, 1), (1, -1), (-1, 1), (-1, -1)]
    for k, j in peers:
        pl.semaphore_signal(
            barrier, inc=1, device_id=(tm(k), rw(j)), device_id_type=pl.DeviceIdType.MESH
        )
    pl.semaphore_wait(barrier, len(peers))

    halos = [
        remote(video.at[pl.ds(2, 2)], raw.at[pl.ds(0, 2), pl.ds(1, BAND)], halo_send.at[0], halo_recv.at[0], 1, 0),
        remote(video.at[:, BAND - 1], raw.at[pl.ds(2, FRAMES), 0], halo_send.at[1], halo_recv.at[1], 0, 1),
        remote(video.at[:, 0], raw.at[pl.ds(2, FRAMES), BAND + 1], halo_send.at[2], halo_recv.at[2], 0, -1),
        remote(video.at[pl.ds(2, 2), BAND - 1], raw.at[pl.ds(0, 2), 0], halo_send.at[3], halo_recv.at[3], 1, 1),
        remote(video.at[pl.ds(2, 2), 0], raw.at[pl.ds(0, 2), BAND + 1], halo_send.at[4], halo_recv.at[4], 1, -1),
    ]
    for copy in halos:
        copy.start()

    for f in range(FRAMES):
        loads[f].wait()

        def add_row(i, sums, f=f):
            x = raw[2 + f, 1 + i].astype(F32).reshape(COLS // 8, 8, CH)
            return sums[0] + jnp.sum(x, axis=0), sums[1] + jnp.sum(x * x, axis=0)

        zero = jnp.zeros((8, CH), F32)
        s, q = lax.fori_loop(0, BAND, add_row, (zero, zero))
        part[pl.ds(f, 1)] = jnp.sum(s, axis=0, keepdims=True)
        part[pl.ds(FRAMES + f, 1)] = jnp.sum(q, axis=0, keepdims=True)

    rcopies = [
        remote(part, rbuf.at[j], r_send.at[j], r_recv.at[j], 0, j) for j in range(1, ROWS)
    ]
    for copy in rcopies:
        copy.start()

    loads[FRAMES].wait()
    loads[FRAMES + 1].wait()

    def lay_conv(a, carry):
        for rr in range(4):
            for e in range(3):
                at = pl.ds((rr * 3 + e) * CH, CH)
                empty = jnp.zeros((CH, CH), BF16)
                wc[a, at, pl.ds(0, CH)] = cw[a, rr, e] if rr < 3 else empty
                wc[a, at, pl.ds(CH, CH)] = cw[a, rr - 1, e] if rr > 0 else empty
        return carry

    lax.fori_loop(0, 3, lay_conv, 0)
    for a in range(3):
        for be in range(9):
            wd[pl.ds(be * CH, CH), pl.ds(a * CH, CH)] = dw[a, be // 3, be % 3]

    base = d * FRAMES - 2
    firsts, ends = [], []
    for e in range(EXT + 1):
        first, end, start = jnp.int32(0), jnp.int32(0), jnp.int32(0)
        for c in range(8):
            stop = start + clip[c]
            inside = (base + e >= start) & (base + e < stop)
            first = jnp.where(inside, start, first)
            end = jnp.where(inside, stop, end)
            start = stop
        firsts.append(first - base)
        ends.append(end - base)

    rbuf[0] = part[...]
    for copy in rcopies:
        copy.wait_recv()
    total = rbuf[0]
    for j in range(1, ROWS):
        total = total + rbuf[j]
    tot[...] = total
    tbuf[2] = total
    tcopies = [
        remote(tot, tbuf.at[2 - k], t_send.at[2 - k], t_recv.at[2 - k], k, 0)
        for k in (-2, -1, 1, 2)
    ]
    for copy in tcopies:
        copy.start()
    for copy in tcopies:
        copy.wait_recv()

    sub = lax.broadcasted_iota(jnp.int32, (8, CH), 0)
    mom[...] = jnp.zeros((16, CH), F32)
    count = jnp.ones((8, CH), F32)
    for e in range(EXT):
        mine = jnp.zeros((8, CH), F32)
        for k in range(5):
            at = lax.rem(sub, FRAMES) + (2 + (k - 2) * FRAMES)
            mine = mine + jnp.where((at >= firsts[e]) & (at < ends[e]), tbuf[k], 0.0)
        mom[pl.ds(e, 1)] = jnp.sum(jnp.where(sub < FRAMES, mine, 0.0), axis=0, keepdims=True)
        mom[pl.ds(8 + e, 1)] = jnp.sum(jnp.where(sub >= FRAMES, mine, 0.0), axis=0, keepdims=True)
        frames = jnp.maximum(ends[e] - firsts[e], 1)
        count = jnp.where(sub == e, (frames * (HEIGHT * COLS * PER_GROUP)).astype(F32), count)
    lane_a = lax.broadcasted_iota(jnp.int32, (CH, CH), 0) // PER_GROUP
    lane_b = lax.broadcasted_iota(jnp.int32, (CH, CH), 1) // PER_GROUP
    same = jnp.where(lane_a == lane_b, 1.0, 0.0).astype(F32)
    grouped = jnp.dot(
        mom[...], same, preferred_element_type=F32, precision=lax.Precision.HIGHEST
    )
    mean = grouped[0:8] / count
    scale = lax.rsqrt(grouped[8:16] / count - mean * mean + EPSILON)
    slope = scale * gain[...]
    coef[0] = 0.5 * slope
    coef[1] = 0.5 * (shift[...] - mean * slope)

    def activate(f, n):
        def row(i, carry):
            pick = jnp.where((i == 0) & (r == 0), 1, i)
            pick = jnp.where((i == BAND + 1) & (r == ROWS - 1), BAND, pick)
            x = raw[f, pick].astype(F32)
            h = x * coef[0, pl.ds(f, 1)] + coef[1, pl.ds(f, 1)]
            v = h * jnp.tanh(h) + h
            hs[pl.ds(8, COLS)] = v
            hs[pl.ds(7, 1)] = v[0:1]
            hs[pl.ds(8 + COLS, 1)] = v[COLS - 1:COLS]
            hid[f, i, :, pl.ds(0, CH)] = hs[pl.ds(7, COLS)].astype(BF16)
            hid[f, i, :, pl.ds(CH, CH)] = v.astype(BF16)
            hid[f, i, :, pl.ds(2 * CH, CH)] = hs[pl.ds(9, COLS)].astype(BF16)
            return carry

        lax.fori_loop(0, BAND + 2, row, 0)

    def spread(y, f, row, slot):
        ss[slot, pl.ds(8, COLS)] = y
        ss[slot, pl.ds(7, 1)] = y[0:1]
        for e in range(3):
            dn[f, row, :, pl.ds(e * CH, CH)] = ss[slot, pl.ds(7 + e, OUT_COLS, stride=2)].astype(BF16)

    rowcopies = [
        remote(rowsend.at[pl.ds(2, 2)], rowrecv.at[pl.ds(2, 2)], row_send.at[0], row_recv.at[0], 0, 1),
        remote(rowsend.at[pl.ds(0, 2)], rowrecv.at[pl.ds(0, 2)], row_send.at[1], row_recv.at[1], 0, 1),
    ]

    def convolve(pair):
        def step(n, carry):
            p = BAND // 2 - 1 - n
            for f in pair:
                acc = None
                for a in range(3):
                    at = jnp.maximum(f - 2 + a, firsts[f])
                    taps = jnp.concatenate([hid[at, 2 * p + rr] for rr in range(4)], axis=-1)
                    term = jnp.dot(taps, wc[a], preferred_element_type=F32)
                    acc = term if acc is None else acc + term
                for half in range(2):
                    y = acc[:, half * CH:(half + 1) * CH] + cbias[...]
                    y = y + raw[f, 2 * p + 1 + half].astype(F32)
                    spread(y, f - 2, 2 * p + 1 + half, half)
                    if half == 1:
                        @pl.when(n == 0)
                        def _(y=y, f=f):
                            rowsend[f - 2] = y.astype(BF16)

            @pl.when(n == 0)
            def _():
                rowcopies[0 if pair[0] == 4 else 1].start()

            return carry

        lax.fori_loop(0, BAND // 2, step, 0)

    def upper(pair):
        rowcopies[0 if pair[0] == 4 else 1].wait_recv()
        for f in pair:
            spread(rowrecv[f - 2].astype(F32), f - 2, 0, 0)

            @pl.when(r == 0)
            def _(f=f):
                dn[f - 2, 0] = dn[f - 2, 1]

    def downsample(s):
        taps = jnp.concatenate(
            [
                jnp.concatenate([dn[s, 2 * i + b] for b in range(3)], axis=-1)
                for i in range(OUT_ROWS)
            ],
            axis=0,
        )
        z[s] = jnp.dot(taps, wd[...], preferred_element_type=F32)

    lane = [pl.ds(a * CH, CH) for a in range(3)]

    halos[1].wait_recv()
    halos[2].wait_recv()
    for f in range(2, EXT):
        activate(f, BAND + 2)
    convolve((4, 5))
    upper((4, 5))
    downsample(2)
    downsample(3)
    ahead = jnp.minimum(jnp.maximum(firsts[EXT] - 2, 2), 3)
    psend[0] = z[3, :, lane[1]] + z[ahead, :, lane[0]]
    psend[1] = z[3, :, lane[0]]
    pcopy = remote(psend, precv, p_send.at[0], p_recv.at[0], 1, 0)
    pcopy.start()

    for j in (0, 3, 4):
        halos[j].wait_recv()
    for f in range(2):
        activate(f, BAND + 2)
    convolve((2, 3))
    upper((2, 3))
    downsample(0)
    downsample(1)
    pcopy.wait_recv()

    for t in range(FRAMES):
        first = firsts[t + 2] - 2
        total = z[t, :, lane[2]] + dbias[...]
        one = jnp.maximum(jnp.maximum(t - 1, first), 0)
        two = jnp.maximum(jnp.maximum(t - 2, first), 0)
        if t == 0:
            rest = jnp.where(first < 0, precv[0], z[0, :, lane[1]] + z[0, :, lane[0]])
        elif t == 1:
            rest = z[one, :, lane[1]] + jnp.where(first < 0, precv[1], z[two, :, lane[0]])
        else:
            rest = z[one, :, lane[1]] + z[two, :, lane[0]]
        out[t] = (total + rest).astype(BF16).reshape(OUT_ROWS, OUT_COLS, CH)

    for copy in halos + rcopies + tcopies + rowcopies + [pcopy]:
        copy.wait_send()


def per_device(video, clip_lengths, gain, shift, conv_weight, conv_bias, down_weight, down_bias):
    any_space = pl.BlockSpec(memory_space=pl.ANY)
    vmem = pl.BlockSpec(memory_space=pltpu.VMEM)
    smem = pl.BlockSpec(memory_space=pltpu.SMEM)
    dma = pltpu.SemaphoreType.DMA
    pixels = OUT_ROWS * OUT_COLS
    return pl.pallas_call(
        kernel,
        out_shape=jax.ShapeDtypeStruct((FRAMES, OUT_ROWS, OUT_COLS, CH), BF16),
        in_specs=[any_space, smem, vmem, vmem, any_space, vmem, any_space, vmem],
        out_specs=vmem,
        scratch_shapes=[
            pltpu.VMEM((EXT, BAND + 2, COLS, CH), BF16),
            pltpu.VMEM((EXT, BAND + 2, COLS, 3 * CH), BF16),
            pltpu.VMEM((3, 3, 3, CH, CH), BF16),
            pltpu.VMEM((3, 3, 3, CH, CH), BF16),
            pltpu.VMEM((3, 12 * CH, 2 * CH), BF16),
            pltpu.VMEM((9 * CH, 3 * CH), BF16),
            pltpu.VMEM((8, CH), F32),
            pltpu.VMEM((8, CH), F32),
            pltpu.VMEM((ROWS, 8, CH), F32),
            pltpu.VMEM((5, 8, CH), F32),
            pltpu.VMEM((16, CH), F32),
            pltpu.VMEM((2, 8, CH), F32),
            pltpu.VMEM((COLS + 16, CH), F32),
            pltpu.VMEM((2, COLS + 8, CH), F32),
            pltpu.VMEM((FRAMES, BAND + 1, OUT_COLS, 3 * CH), BF16),
            pltpu.VMEM((FRAMES, COLS, CH), BF16),
            pltpu.VMEM((FRAMES, COLS, CH), BF16),
            pltpu.VMEM((FRAMES, pixels, 3 * CH), F32),
            pltpu.VMEM((2, pixels, CH), F32),
            pltpu.VMEM((2, pixels, CH), F32),
            dma((FRAMES + 2,)),
            dma((5,)), dma((5,)),
            dma((ROWS,)), dma((ROWS,)),
            dma((5,)), dma((5,)),
            dma((2,)), dma((2,)),
            dma((1,)), dma((1,)),
        ],
        compiler_params=pltpu.CompilerParams(
            collective_id=0, has_side_effects=True, vmem_limit_bytes=56 * 1024 * 1024
        ),
        cost_estimate=pl.CostEstimate(
            flops=9_060_000_000, bytes_accessed=5_000_000, transcendentals=2_000_000
        ),
        name="encode",
    )(
        video, clip_lengths, gain.reshape(1, CH), shift.reshape(1, CH),
        conv_weight, conv_bias.reshape(1, CH), down_weight, down_bias.reshape(1, CH),
    )


def solution(mesh):
    placed = (P("tm", "rows", None, None), P(), P(), P(), P(), P(), P(), P())
    return jax.shard_map(
        per_device, mesh=mesh, in_specs=placed,
        out_specs=P("tm", "rows", None, None), check_vma=False,
    )
```

```python
import jax
import jax.numpy as jnp
from jax import lax
from jax.experimental import pallas as pl
from jax.experimental.pallas import tpu as pltpu
from jax.sharding import PartitionSpec as P

GROUPS = 32
EPSILON = 1e-06
TM, ROWS = 8, 16
FRAMES, BAND, COLS, CH = 4, 8, 256, 128
HEIGHT = BAND * ROWS
PER_GROUP = CH // GROUPS
EXT = FRAMES + 2
OUT_ROWS, OUT_COLS = BAND // 2, COLS // 2
F32, BF16 = jnp.float32, jnp.bfloat16


def kernel(
    video, clip, gain, shift, cw_hbm, cbias, dw_hbm, dbias, out,
    raw, hid0, hid1, hid2, hid3, hid4, cw, dw, wc, wd, part, tot, rbuf, tbuf, mom, coef, hs, ss, dn,
    rowsend, rowrecv, z, psend, precv,
    load_sem, halo_send, halo_recv, r_send, r_recv, t_send, t_recv,
    row_send, row_recv, p_send, p_recv,
):
    hid = (hid0, hid1, hid2, hid3, hid4)
    d = lax.axis_index("tm")
    r = lax.axis_index("rows")

    def tm(k):
        return lax.rem(d + (k + TM), TM)

    def rw(k):
        return lax.rem(r + (k + ROWS), ROWS)

    def remote(src, dst, send, recv, k, j):
        return pltpu.make_async_remote_copy(
            src_ref=src, dst_ref=dst, send_sem=send, recv_sem=recv,
            device_id=(tm(k), rw(j)), device_id_type=pl.DeviceIdType.MESH,
        )

    loads = [
        pltpu.make_async_copy(video.at[f], raw.at[2 + f, pl.ds(1, BAND)], load_sem.at[f])
        for f in range(FRAMES)
    ]
    loads.append(pltpu.make_async_copy(cw_hbm, cw, load_sem.at[FRAMES]))
    loads.append(pltpu.make_async_copy(dw_hbm, dw, load_sem.at[FRAMES + 1]))
    for copy in loads:
        copy.start()

    barrier = pltpu.get_barrier_semaphore()
    peers = [(0, j) for j in range(1, ROWS)] + [(k, 0) for k in (-2, -1, 1, 2)]
    peers += [(1, 1), (1, -1), (-1, 1), (-1, -1)]
    for k, j in peers:
        pl.semaphore_signal(
            barrier, inc=1, device_id=(tm(k), rw(j)), device_id_type=pl.DeviceIdType.MESH
        )

    for f in range(FRAMES):
        loads[f].wait()

        def add_row(i, sums, f=f):
            x = raw[2 + f, 1 + i].astype(F32).reshape(COLS // 8, 8, CH)
            return sums[0] + jnp.sum(x, axis=0), sums[1] + jnp.sum(x * x, axis=0)

        zero = jnp.zeros((8, CH), F32)
        s, q = lax.fori_loop(0, BAND, add_row, (zero, zero))
        part[pl.ds(f, 1)] = jnp.sum(s, axis=0, keepdims=True)
        part[pl.ds(FRAMES + f, 1)] = jnp.sum(q, axis=0, keepdims=True)

    loads[FRAMES].wait()
    loads[FRAMES + 1].wait()

    def lay_conv(a, carry):
        for rr in range(4):
            for e in range(3):
                at = pl.ds((rr * 3 + e) * CH, CH)
                empty = jnp.zeros((CH, CH), BF16)
                wc[a, at, pl.ds(0, CH)] = cw[a, rr, e] if rr < 3 else empty
                wc[a, at, pl.ds(CH, CH)] = cw[a, rr - 1, e] if rr > 0 else empty
        return carry

    lax.fori_loop(0, 3, lay_conv, 0)
    for a in range(3):
        for be in range(9):
            wd[pl.ds(be * CH, CH), pl.ds(a * CH, CH)] = dw[a, be // 3, be % 3]

    base = d * FRAMES - 2
    firsts, ends = [], []
    for e in range(EXT + 1):
        first, end, start = jnp.int32(0), jnp.int32(0), jnp.int32(0)
        for c in range(8):
            stop = start + clip[c]
            inside = (base + e >= start) & (base + e < stop)
            first = jnp.where(inside, start, first)
            end = jnp.where(inside, stop, end)
            start = stop
        firsts.append(first - base)
        ends.append(end - base)

    pl.semaphore_wait(barrier, len(peers))

    rcopies = [
        remote(part, rbuf.at[j], r_send.at[j], r_recv.at[j], 0, j) for j in range(1, ROWS)
    ]
    for copy in rcopies:
        copy.start()

    halos = [
        remote(video.at[pl.ds(2, 2)], raw.at[pl.ds(0, 2), pl.ds(1, BAND)], halo_send.at[0], halo_recv.at[0], 1, 0),
        remote(video.at[:, BAND - 1], raw.at[pl.ds(2, FRAMES), 0], halo_send.at[1], halo_recv.at[1], 0, 1),
        remote(video.at[:, 0], raw.at[pl.ds(2, FRAMES), BAND + 1], halo_send.at[2], halo_recv.at[2], 0, -1),
        remote(video.at[pl.ds(2, 2), BAND - 1], raw.at[pl.ds(0, 2), 0], halo_send.at[3], halo_recv.at[3], 1, 1),
        remote(video.at[pl.ds(2, 2), 0], raw.at[pl.ds(0, 2), BAND + 1], halo_send.at[4], halo_recv.at[4], 1, -1),
    ]
    for copy in halos:
        copy.start()

    rbuf[0] = part[...]
    for copy in rcopies:
        copy.wait_recv()
    total = rbuf[0]
    for j in range(1, ROWS):
        total = total + rbuf[j]
    tot[...] = total
    tbuf[2] = total
    tcopies = [
        remote(tot, tbuf.at[2 - k], t_send.at[2 - k], t_recv.at[2 - k], k, 0)
        for k in (-2, -1, 1, 2)
    ]
    for copy in tcopies:
        copy.start()
    for copy in tcopies:
        copy.wait_recv()

    sub = lax.broadcasted_iota(jnp.int32, (8, CH), 0)
    mom[...] = jnp.zeros((16, CH), F32)
    count = jnp.ones((8, CH), F32)
    for e in range(EXT):
        mine = jnp.zeros((8, CH), F32)
        for k in range(5):
            at = lax.rem(sub, FRAMES) + (2 + (k - 2) * FRAMES)
            mine = mine + jnp.where((at >= firsts[e]) & (at < ends[e]), tbuf[k], 0.0)
        mom[pl.ds(e, 1)] = jnp.sum(jnp.where(sub < FRAMES, mine, 0.0), axis=0, keepdims=True)
        mom[pl.ds(8 + e, 1)] = jnp.sum(jnp.where(sub >= FRAMES, mine, 0.0), axis=0, keepdims=True)
        frames = jnp.maximum(ends[e] - firsts[e], 1)
        count = jnp.where(sub == e, (frames * (HEIGHT * COLS * PER_GROUP)).astype(F32), count)
    lane_a = lax.broadcasted_iota(jnp.int32, (CH, CH), 0) // PER_GROUP
    lane_b = lax.broadcasted_iota(jnp.int32, (CH, CH), 1) // PER_GROUP
    same = jnp.where(lane_a == lane_b, 1.0, 0.0).astype(F32)
    grouped = jnp.dot(
        mom[...], same, preferred_element_type=F32, precision=lax.Precision.HIGHEST
    )
    mean = grouped[0:8] / count
    scale = lax.rsqrt(grouped[8:16] / count - mean * mean + EPSILON)
    slope = scale * gain[...]
    coef[0] = 0.5 * slope
    coef[1] = 0.5 * (shift[...] - mean * slope)

    def activate(frames, group):
        for f in frames:
            for q in range(2):
                i = 2 * group + q
                pick = i
                if i == 0:
                    pick = jnp.where(r == 0, 1, 0)
                if i == BAND + 1:
                    pick = jnp.where(r == ROWS - 1, BAND, BAND + 1)
                x = raw[f, pick].astype(F32)
                h = x * coef[0, pl.ds(f, 1)] + coef[1, pl.ds(f, 1)]
                v = h * jnp.tanh(h) + h
                slot = 2 * (f % 2) + q
                hs[slot, pl.ds(8, COLS)] = v
                hs[slot, pl.ds(7, 1)] = v[0:1]
                hs[slot, pl.ds(8 + COLS, 1)] = v[COLS - 1:COLS]
                hid[group][f, q, :, pl.ds(0, CH)] = hs[slot, pl.ds(7, COLS)].astype(BF16)
                hid[group][f, q, :, pl.ds(CH, CH)] = v.astype(BF16)
                hid[group][f, q, :, pl.ds(2 * CH, CH)] = hs[slot, pl.ds(9, COLS)].astype(BF16)

    def spread(y, f, row, slot):
        ss[slot, pl.ds(8, COLS)] = y
        ss[slot, pl.ds(7, 1)] = y[0:1]
        for e in range(3):
            dn[f, row, :, pl.ds(e * CH, CH)] = ss[slot, pl.ds(7 + e, OUT_COLS, stride=2)].astype(BF16)

    rowcopies = [
        remote(rowsend.at[pl.ds(2, 2)], rowrecv.at[pl.ds(2, 2)], row_send.at[0], row_recv.at[0], 0, 1),
        remote(rowsend.at[pl.ds(0, 2)], rowrecv.at[pl.ds(0, 2)], row_send.at[1], row_recv.at[1], 0, 1),
    ]

    def convolve(f, p):
        acc = None
        for a in range(3):
            at = jnp.maximum(f - 2 + a, firsts[f])
            taps = jnp.concatenate(
                [hid[p][at, 0], hid[p][at, 1], hid[p + 1][at, 0], hid[p + 1][at, 1]], axis=-1
            )
            term = jnp.dot(taps, wc[a], preferred_element_type=F32)
            acc = term if acc is None else acc + term
        for half in range(2):
            y = acc[:, half * CH:(half + 1) * CH] + cbias[...]
            y = y + raw[f, 2 * p + 1 + half].astype(F32)
            spread(y, f - 2, 2 * p + 1 + half, half)
            if p == BAND // 2 - 1 and half == 1:
                rowsend[f - 2] = y.astype(BF16)

    def upper(pair):
        for f in pair:
            spread(rowrecv[f - 2].astype(F32), f - 2, 0, 0)

            @pl.when(r == 0)
            def _(f=f):
                dn[f - 2, 0] = dn[f - 2, 1]

    def downsample(frames, rows):
        taps = jnp.concatenate(
            [
                jnp.concatenate([dn[s, 2 * i + b] for b in range(3)], axis=-1)
                for s in frames
                for i in rows
            ],
            axis=0,
        )
        res = jnp.dot(taps, wd[...], preferred_element_type=F32)
        n = len(rows) * OUT_COLS
        for k, s in enumerate(frames):
            z[s, pl.ds(rows[0] * OUT_COLS, n)] = res[k * n:(k + 1) * n]

    def partial_sums(start, n):
        at = pl.ds(start, n)
        psend[0, at] = z[3, at, lane[1]] + z[ahead, at, lane[0]]
        psend[1, at] = z[3, at, lane[0]]

    lane = [pl.ds(a * CH, CH) for a in range(3)]

    ahead = jnp.minimum(jnp.maximum(firsts[EXT] - 2, 2), 3)
    own, late, early, before = (2, 3, 4, 5), (4, 5), (2, 3), (0, 1)
    top, rest = pl.ds(0, OUT_COLS), pl.ds(OUT_COLS, 3 * OUT_COLS)
    pcopies = [
        remote(psend.at[:, rest], precv.at[:, rest], p_send.at[0], p_recv.at[0], 1, 0),
        remote(psend.at[:, top], precv.at[:, top], p_send.at[1], p_recv.at[1], 1, 0),
    ]

    halos[2].wait_recv()
    activate(own, 4)
    activate(own, 3)
    for f in late:
        convolve(f, 3)
    activate(own, 2)
    rowcopies[0].start()
    for f in late:
        convolve(f, 2)
    activate(own, 1)
    halos[1].wait_recv()
    for f in late:
        convolve(f, 1)
    activate(own, 0)
    for f in late:
        convolve(f, 0)
    downsample((2, 3), (1, 2, 3))
    partial_sums(OUT_COLS, 3 * OUT_COLS)
    pcopies[0].start()

    for j in (0, 3, 4):
        halos[j].wait_recv()
    activate(before, 4)
    activate(before, 3)
    for f in early:
        convolve(f, 3)
    activate(before, 2)
    rowcopies[1].start()
    rowcopies[0].wait_recv()
    upper(late)
    downsample((2, 3), (0,))
    partial_sums(0, OUT_COLS)
    pcopies[1].start()
    for f in early:
        convolve(f, 2)
    activate(before, 1)
    for f in early:
        convolve(f, 1)
    activate(before, 0)
    for f in early:
        convolve(f, 0)
    downsample((0, 1), (1, 2, 3))
    rowcopies[1].wait_recv()
    upper(early)
    downsample((0, 1), (0,))
    for copy in pcopies:
        copy.wait_recv()

    for t in range(FRAMES):
        first = firsts[t + 2] - 2
        total = z[t, :, lane[2]] + dbias[...]
        one = jnp.maximum(jnp.maximum(t - 1, first), 0)
        two = jnp.maximum(jnp.maximum(t - 2, first), 0)
        if t == 0:
            rest = jnp.where(first < 0, precv[0], z[0, :, lane[1]] + z[0, :, lane[0]])
        elif t == 1:
            rest = z[one, :, lane[1]] + jnp.where(first < 0, precv[1], z[two, :, lane[0]])
        else:
            rest = z[one, :, lane[1]] + z[two, :, lane[0]]
        out[t] = (total + rest).astype(BF16).reshape(OUT_ROWS, OUT_COLS, CH)

    for copy in halos + rcopies + tcopies + rowcopies + pcopies:
        copy.wait_send()


def per_device(video, clip_lengths, gain, shift, conv_weight, conv_bias, down_weight, down_bias):
    any_space = pl.BlockSpec(memory_space=pl.ANY)
    vmem = pl.BlockSpec(memory_space=pltpu.VMEM)
    smem = pl.BlockSpec(memory_space=pltpu.SMEM)
    dma = pltpu.SemaphoreType.DMA
    pixels = OUT_ROWS * OUT_COLS
    return pl.pallas_call(
        kernel,
        out_shape=jax.ShapeDtypeStruct((FRAMES, OUT_ROWS, OUT_COLS, CH), BF16),
        in_specs=[any_space, smem, vmem, vmem, any_space, vmem, any_space, vmem],
        out_specs=vmem,
        scratch_shapes=[
            pltpu.VMEM((EXT, BAND + 2, COLS, CH), BF16),
            *[pltpu.VMEM((EXT, 2, COLS, 3 * CH), BF16)] * 5,
            pltpu.VMEM((3, 3, 3, CH, CH), BF16),
            pltpu.VMEM((3, 3, 3, CH, CH), BF16),
            pltpu.VMEM((3, 12 * CH, 2 * CH), BF16),
            pltpu.VMEM((9 * CH, 3 * CH), BF16),
            pltpu.VMEM((8, CH), F32),
            pltpu.VMEM((8, CH), F32),
            pltpu.VMEM((ROWS, 8, CH), F32),
            pltpu.VMEM((5, 8, CH), F32),
            pltpu.VMEM((16, CH), F32),
            pltpu.VMEM((2, 8, CH), F32),
            pltpu.VMEM((4, COLS + 16, CH), F32),
            pltpu.VMEM((2, COLS + 8, CH), F32),
            pltpu.VMEM((FRAMES, BAND + 1, OUT_COLS, 3 * CH), BF16),
            pltpu.VMEM((FRAMES, COLS, CH), BF16),
            pltpu.VMEM((FRAMES, COLS, CH), BF16),
            pltpu.VMEM((FRAMES, pixels, 3 * CH), F32),
            pltpu.VMEM((2, pixels, CH), F32),
            pltpu.VMEM((2, pixels, CH), F32),
            dma((FRAMES + 2,)),
            dma((5,)), dma((5,)),
            dma((ROWS,)), dma((ROWS,)),
            dma((5,)), dma((5,)),
            dma((2,)), dma((2,)),
            dma((2,)), dma((2,)),
        ],
        compiler_params=pltpu.CompilerParams(
            collective_id=0, has_side_effects=True, vmem_limit_bytes=56 * 1024 * 1024
        ),
        cost_estimate=pl.CostEstimate(
            flops=9_060_000_000, bytes_accessed=5_000_000, transcendentals=2_000_000
        ),
        name="encode",
    )(
        video, clip_lengths, gain.reshape(1, CH), shift.reshape(1, CH),
        conv_weight, conv_bias.reshape(1, CH), down_weight, down_bias.reshape(1, CH),
    )


def solution(mesh):
    placed = (P("tm", "rows", None, None), P(), P(), P(), P(), P(), P(), P())
    return jax.shard_map(
        per_device, mesh=mesh, in_specs=placed,
        out_specs=P("tm", "rows", None, None), check_vma=False,
    )
```

```python
import jax
import jax.numpy as jnp
from jax import lax
from jax.experimental import pallas as pl
from jax.experimental.pallas import tpu as pltpu
from jax.sharding import PartitionSpec as P

GROUPS = 32
EPSILON = 1e-06
TM, ROWS = 8, 16
FRAMES, BAND, COLS, CH = 4, 8, 256, 128
HEIGHT = BAND * ROWS
PER_GROUP = CH // GROUPS
EXT = FRAMES + 2
OUT_ROWS, OUT_COLS = BAND // 2, COLS // 2
F32, BF16 = jnp.float32, jnp.bfloat16


def kernel(
    video, clip_hbm, gain_hbm, shift_hbm, cw_hbm, cbias_hbm, dw_hbm, dbias_hbm, out,
    clip, gain, shift, cbias, dbias, raw, hid0, hid1, hid2, hid3, hid4, cw, dw, wc, wd, part, rbuf, tbuf, mom, coef, hs, ss, dn,
    rowsend, rowrecv, z, psend, precv,
    load_sem, halo_send, halo_recv, r_send, r_recv, t_send, t_recv,
    row_send, row_recv, p_send, p_recv,
):
    hid = (hid0, hid1, hid2, hid3, hid4)
    d = lax.axis_index("tm")
    r = lax.axis_index("rows")

    def tm(k):
        return lax.rem(d + (k + TM), TM)

    def rw(k):
        return lax.rem(r + (k + ROWS), ROWS)

    def remote(src, dst, send, recv, k, j):
        return pltpu.make_async_remote_copy(
            src_ref=src, dst_ref=dst, send_sem=send, recv_sem=recv,
            device_id=(tm(k), rw(j)), device_id_type=pl.DeviceIdType.MESH,
        )

    loads = [
        pltpu.make_async_copy(video.at[f], raw.at[2 + f, pl.ds(1, BAND)], load_sem.at[f])
        for f in range(FRAMES)
    ]
    loads.append(pltpu.make_async_copy(cw_hbm, cw, load_sem.at[FRAMES]))
    loads.append(pltpu.make_async_copy(dw_hbm, dw, load_sem.at[FRAMES + 1]))
    small = [(clip_hbm, clip), (gain_hbm, gain), (shift_hbm, shift), (cbias_hbm, cbias), (dbias_hbm, dbias)]
    for n, (source, target) in enumerate(small):
        loads.append(pltpu.make_async_copy(source, target, load_sem.at[FRAMES + 2 + n]))
    for copy in loads:
        copy.start()

    barrier = pltpu.get_barrier_semaphore()
    peers = [(0, j) for j in range(1, ROWS)] + [(k, 0) for k in (-2, -1, 1, 2)]
    peers += [(1, 1), (1, -1), (-1, 1), (-1, -1)]
    for k, j in peers:
        pl.semaphore_signal(
            barrier, inc=1, device_id=(tm(k), rw(j)), device_id_type=pl.DeviceIdType.MESH
        )

    for f in range(FRAMES):
        loads[f].wait()

        def add_row(i, sums, f=f):
            x = raw[2 + f, 1 + i].astype(F32).reshape(COLS // 8, 8, CH)
            return sums[0] + jnp.sum(x, axis=0), sums[1] + jnp.sum(x * x, axis=0)

        zero = jnp.zeros((8, CH), F32)
        s, q = lax.fori_loop(0, BAND, add_row, (zero, zero))
        part[pl.ds(f, 1)] = jnp.sum(s, axis=0, keepdims=True)
        part[pl.ds(FRAMES + f, 1)] = jnp.sum(q, axis=0, keepdims=True)

    pl.semaphore_wait(barrier, len(peers))

    tbuf[2] = part[...]
    tcopies = [
        remote(part, tbuf.at[2 - k], t_send.at[2 - k], t_recv.at[2 - k], k, 0)
        for k in (1, 2, -1, -2)
    ]
    for copy in tcopies:
        copy.start()
    halos = [
        remote(video.at[pl.ds(2, 2), pl.ds(4, 4)], raw.at[pl.ds(0, 2), pl.ds(5, 4)], halo_send.at[0], halo_recv.at[0], 1, 0),
        remote(video.at[:, BAND - 1], raw.at[pl.ds(2, FRAMES), 0], halo_send.at[1], halo_recv.at[1], 0, 1),
        remote(video.at[pl.ds(0, 2), 0], raw.at[pl.ds(2, 2), BAND + 1], halo_send.at[2], halo_recv.at[2], 0, -1),
        remote(video.at[pl.ds(2, 2), BAND - 1], raw.at[pl.ds(0, 2), 0], halo_send.at[3], halo_recv.at[3], 1, 1),
        remote(video.at[pl.ds(2, 2), 0], raw.at[pl.ds(0, 2), BAND + 1], halo_send.at[4], halo_recv.at[4], 1, -1),
        remote(video.at[pl.ds(2, 2), pl.ds(0, 4)], raw.at[pl.ds(0, 2), pl.ds(1, 4)], halo_send.at[5], halo_recv.at[5], 1, 0),
        remote(video.at[pl.ds(2, 2), 0], raw.at[pl.ds(4, 2), BAND + 1], halo_send.at[6], halo_recv.at[6], 0, -1),
    ]
    halos[2].start()
    halos[0].start()

    for copy in loads[FRAMES + 2:]:
        copy.wait()

    base = d * FRAMES - 2
    firsts, ends = [], []
    for e in range(EXT + 1):
        first, end, start = jnp.int32(0), jnp.int32(0), jnp.int32(0)
        for c in range(8):
            stop = start + clip[c]
            inside = (base + e >= start) & (base + e < stop)
            first = jnp.where(inside, start, first)
            end = jnp.where(inside, stop, end)
            start = stop
        firsts.append(first - base)
        ends.append(end - base)
    sub = lax.broadcasted_iota(jnp.int32, (8, CH), 0)
    count = jnp.ones((8, CH), F32)
    for e in range(EXT):
        frames = jnp.maximum(ends[e] - firsts[e], 1)
        count = jnp.where(sub == e, (frames * (HEIGHT * COLS * PER_GROUP)).astype(F32), count)

    for copy in tcopies:
        copy.wait_recv()
    mom[...] = jnp.zeros((16, CH), F32)
    for e in range(EXT):
        mine = jnp.zeros((8, CH), F32)
        for k in range(5):
            at = lax.rem(sub, FRAMES) + (2 + (k - 2) * FRAMES)
            mine = mine + jnp.where((at >= firsts[e]) & (at < ends[e]), tbuf[k], 0.0)
        mom[pl.ds(e, 1)] = jnp.sum(jnp.where(sub < FRAMES, mine, 0.0), axis=0, keepdims=True)
        mom[pl.ds(8 + e, 1)] = jnp.sum(jnp.where(sub >= FRAMES, mine, 0.0), axis=0, keepdims=True)
    rcopies = [
        remote(mom, rbuf.at[j], r_send.at[j], r_recv.at[j], 0, j) for j in range(1, ROWS)
    ]
    for copy in rcopies:
        copy.start()
    for j in (6, 1, 4, 5, 3):
        halos[j].start()

    loads[FRAMES].wait()
    loads[FRAMES + 1].wait()

    def lay_conv(a, carry):
        for rr in range(4):
            for e in range(3):
                at = pl.ds((rr * 3 + e) * CH, CH)
                empty = jnp.zeros((CH, CH), BF16)
                wc[a, at, pl.ds(0, CH)] = cw[a, rr, e] if rr < 3 else empty
                wc[a, at, pl.ds(CH, CH)] = cw[a, rr - 1, e] if rr > 0 else empty
        return carry

    lax.fori_loop(0, 3, lay_conv, 0)
    for a in range(3):
        for be in range(9):
            wd[pl.ds(be * CH, CH), pl.ds(a * CH, CH)] = dw[a, be // 3, be % 3]
    lane_a = lax.broadcasted_iota(jnp.int32, (CH, CH), 0) // PER_GROUP
    lane_b = lax.broadcasted_iota(jnp.int32, (CH, CH), 1) // PER_GROUP
    same = jnp.where(lane_a == lane_b, 1.0, 0.0).astype(F32)

    for copy in rcopies:
        copy.wait_recv()
    total = mom[...]
    for j in range(1, ROWS):
        total = total + rbuf[j]
    grouped = jnp.dot(total, same, preferred_element_type=F32, precision=lax.Precision.HIGHEST)
    mean = grouped[0:8] / count
    scale = lax.rsqrt(grouped[8:16] / count - mean * mean + EPSILON)
    slope = scale * gain[...]
    coef[0] = 0.5 * slope
    coef[1] = 0.5 * (shift[...] - mean * slope)

    def activate(frames, group):
        for f in frames:
            for q in range(2):
                i = 2 * group + q
                pick = i
                if i == 0:
                    pick = jnp.where(r == 0, 1, 0)
                if i == BAND + 1:
                    pick = jnp.where(r == ROWS - 1, BAND, BAND + 1)
                x = raw[f, pick].astype(F32)
                h = x * coef[0, pl.ds(f, 1)] + coef[1, pl.ds(f, 1)]
                v = h * jnp.tanh(h) + h
                slot = 2 * (f % 2) + q
                hs[slot, pl.ds(8, COLS)] = v
                hs[slot, pl.ds(7, 1)] = v[0:1]
                hs[slot, pl.ds(8 + COLS, 1)] = v[COLS - 1:COLS]
                hid[group][f, q, :, pl.ds(0, CH)] = hs[slot, pl.ds(7, COLS)].astype(BF16)
                hid[group][f, q, :, pl.ds(CH, CH)] = v.astype(BF16)
                hid[group][f, q, :, pl.ds(2 * CH, CH)] = hs[slot, pl.ds(9, COLS)].astype(BF16)

    def spread(y, f, row, slot):
        ss[slot, pl.ds(8, COLS)] = y
        ss[slot, pl.ds(7, 1)] = y[0:1]
        for e in range(3):
            dn[f, row, :, pl.ds(e * CH, CH)] = ss[slot, pl.ds(7 + e, OUT_COLS, stride=2)].astype(BF16)

    rowcopies = [
        remote(rowsend.at[pl.ds(2, 2)], rowrecv.at[pl.ds(2, 2)], row_send.at[0], row_recv.at[0], 0, 1),
        remote(rowsend.at[pl.ds(0, 2)], rowrecv.at[pl.ds(0, 2)], row_send.at[1], row_recv.at[1], 0, 1),
    ]

    def convolve(f, p):
        acc = None
        for a in range(3):
            at = jnp.maximum(f - 2 + a, firsts[f])
            taps = jnp.concatenate(
                [hid[p][at, 0], hid[p][at, 1], hid[p + 1][at, 0], hid[p + 1][at, 1]], axis=-1
            )
            term = jnp.dot(taps, wc[a], preferred_element_type=F32)
            acc = term if acc is None else acc + term
        for half in range(2):
            y = acc[:, half * CH:(half + 1) * CH] + cbias[...]
            y = y + raw[f, 2 * p + 1 + half].astype(F32)
            spread(y, f - 2, 2 * p + 1 + half, half)
            if p == BAND // 2 - 1 and half == 1:
                rowsend[f - 2] = y.astype(BF16)

    def upper(pair):
        for f in pair:
            spread(rowrecv[f - 2].astype(F32), f - 2, 0, 0)

            @pl.when(r == 0)
            def _(f=f):
                dn[f - 2, 0] = dn[f - 2, 1]

    def downsample(frames, rows):
        taps = jnp.concatenate(
            [
                jnp.concatenate([dn[s, 2 * i + b] for b in range(3)], axis=-1)
                for s in frames
                for i in rows
            ],
            axis=0,
        )
        res = jnp.dot(taps, wd[...], preferred_element_type=F32)
        n = len(rows) * OUT_COLS
        for k, s in enumerate(frames):
            z[s, pl.ds(rows[0] * OUT_COLS, n)] = res[k * n:(k + 1) * n]

    def partial_sums(start, n):
        at = pl.ds(start, n)
        psend[0, at] = z[3, at, lane[1]] + z[ahead, at, lane[0]]
        psend[1, at] = z[3, at, lane[0]]

    lane = [pl.ds(a * CH, CH) for a in range(3)]

    ahead = jnp.minimum(jnp.maximum(firsts[EXT] - 2, 2), 3)
    own, late, early, before = (2, 3, 4, 5), (4, 5), (2, 3), (0, 1)
    top, rest = pl.ds(0, OUT_COLS), pl.ds(OUT_COLS, 3 * OUT_COLS)
    pcopies = [
        remote(psend.at[:, rest], precv.at[:, rest], p_send.at[0], p_recv.at[0], 1, 0),
        remote(psend.at[:, top], precv.at[:, top], p_send.at[1], p_recv.at[1], 1, 0),
    ]

    halos[2].wait_recv()
    halos[6].wait_recv()
    activate(own, 4)
    activate(own, 3)
    for f in late:
        convolve(f, 3)
    activate(own, 2)
    rowcopies[0].start()
    for f in late:
        convolve(f, 2)
    activate(own, 1)
    halos[1].wait_recv()
    for f in late:
        convolve(f, 1)
    activate(own, 0)
    for f in late:
        convolve(f, 0)
    downsample((2, 3), (1, 2, 3))
    partial_sums(OUT_COLS, 3 * OUT_COLS)
    pcopies[0].start()

    halos[0].wait_recv()
    halos[4].wait_recv()
    activate(before, 4)
    activate(before, 3)
    for f in early:
        convolve(f, 3)
    halos[5].wait_recv()
    activate(before, 2)
    rowcopies[1].start()
    rowcopies[0].wait_recv()
    upper(late)
    downsample((2, 3), (0,))
    partial_sums(0, OUT_COLS)
    pcopies[1].start()
    for f in early:
        convolve(f, 2)
    activate(before, 1)
    for f in early:
        convolve(f, 1)
    halos[3].wait_recv()
    activate(before, 0)
    for f in early:
        convolve(f, 0)
    downsample((0, 1), (1, 2, 3))
    rowcopies[1].wait_recv()
    upper(early)
    downsample((0, 1), (0,))
    for copy in pcopies:
        copy.wait_recv()

    for t in range(FRAMES):
        first = firsts[t + 2] - 2
        total = z[t, :, lane[2]] + dbias[...]
        one = jnp.maximum(jnp.maximum(t - 1, first), 0)
        two = jnp.maximum(jnp.maximum(t - 2, first), 0)
        if t == 0:
            rest = jnp.where(first < 0, precv[0], z[0, :, lane[1]] + z[0, :, lane[0]])
        elif t == 1:
            rest = z[one, :, lane[1]] + jnp.where(first < 0, precv[1], z[two, :, lane[0]])
        else:
            rest = z[one, :, lane[1]] + z[two, :, lane[0]]
        out[t] = (total + rest).astype(BF16).reshape(OUT_ROWS, OUT_COLS, CH)

    for copy in halos + rcopies + tcopies + rowcopies + pcopies:
        copy.wait_send()


def per_device(video, clip_lengths, gain, shift, conv_weight, conv_bias, down_weight, down_bias):
    hbm = pl.BlockSpec(memory_space=pltpu.HBM)
    vmem = pl.BlockSpec(memory_space=pltpu.VMEM)
    dma = pltpu.SemaphoreType.DMA
    pixels = OUT_ROWS * OUT_COLS
    return pl.pallas_call(
        kernel,
        out_shape=jax.ShapeDtypeStruct((FRAMES, OUT_ROWS, OUT_COLS, CH), BF16),
        in_specs=[hbm] * 8,
        out_specs=vmem,
        scratch_shapes=[
            pltpu.SMEM((8,), jnp.int32),
            *[pltpu.VMEM((1, CH), F32)] * 4,
            pltpu.VMEM((EXT, BAND + 2, COLS, CH), BF16),
            *[pltpu.VMEM((EXT, 2, COLS, 3 * CH), BF16)] * 5,
            pltpu.VMEM((3, 3, 3, CH, CH), BF16),
            pltpu.VMEM((3, 3, 3, CH, CH), BF16),
            pltpu.VMEM((3, 12 * CH, 2 * CH), BF16),
            pltpu.VMEM((9 * CH, 3 * CH), BF16),
            pltpu.VMEM((8, CH), F32),
            pltpu.VMEM((ROWS, 16, CH), F32),
            pltpu.VMEM((5, 8, CH), F32),
            pltpu.VMEM((16, CH), F32),
            pltpu.VMEM((2, 8, CH), F32),
            pltpu.VMEM((4, COLS + 16, CH), F32),
            pltpu.VMEM((2, COLS + 8, CH), F32),
            pltpu.VMEM((FRAMES, BAND + 1, OUT_COLS, 3 * CH), BF16),
            pltpu.VMEM((FRAMES, COLS, CH), BF16),
            pltpu.VMEM((FRAMES, COLS, CH), BF16),
            pltpu.VMEM((FRAMES, pixels, 3 * CH), F32),
            pltpu.VMEM((2, pixels, CH), F32),
            pltpu.VMEM((2, pixels, CH), F32),
            dma((FRAMES + 7,)),
            dma((7,)), dma((7,)),
            dma((ROWS,)), dma((ROWS,)),
            dma((5,)), dma((5,)),
            dma((2,)), dma((2,)),
            dma((2,)), dma((2,)),
        ],
        compiler_params=pltpu.CompilerParams(
            collective_id=0, has_side_effects=True, vmem_limit_bytes=56 * 1024 * 1024
        ),
        cost_estimate=pl.CostEstimate(
            flops=9_060_000_000, bytes_accessed=5_000_000, transcendentals=2_000_000
        ),
        name="encode",
    )(
        video, clip_lengths, gain.reshape(1, CH), shift.reshape(1, CH),
        conv_weight, conv_bias.reshape(1, CH), down_weight, down_bias.reshape(1, CH),
    )


def solution(mesh):
    placed = (P("tm", "rows", None, None), P(), P(), P(), P(), P(), P(), P())
    return jax.shard_map(
        per_device, mesh=mesh, in_specs=placed,
        out_specs=P("tm", "rows", None, None), check_vma=False,
    )
```

```python
import jax
import jax.numpy as jnp
from jax import lax
from jax.experimental import pallas as pl
from jax.experimental.pallas import tpu as pltpu
from jax.sharding import PartitionSpec as P

GROUPS = 32
EPSILON = 1e-06
TM, ROWS = 8, 16
FRAMES, BAND, COLS, CH = 4, 8, 256, 128
HEIGHT = BAND * ROWS
PER_GROUP = CH // GROUPS
EXT = FRAMES + 2
OUT_ROWS, OUT_COLS = BAND // 2, COLS // 2
F32, BF16 = jnp.float32, jnp.bfloat16


def kernel(
    video, clip_hbm, gain_hbm, shift_hbm, cw_hbm, cbias_hbm, dw_hbm, dbias_hbm, out,
    clip, gain, shift, cbias, dbias, raw, hid0, hid1, hid2, hid3, hid4, cw, dw, wc, wd, part, rbuf, tbuf, mom, coef, hs, ss, dn,
    rowsend, rowrecv, z, psend, precv,
    load_sem, halo_send, halo_recv, r_send, r_recv, t_send, t_recv,
    row_send, row_recv, p_send, p_recv,
):
    hid = (hid0, hid1, hid2, hid3, hid4)
    d = lax.axis_index("tm")
    r = lax.axis_index("rows")

    def tm(k):
        return lax.rem(d + (k + TM), TM)

    def rw(k):
        return lax.rem(r + (k + ROWS), ROWS)

    def remote(src, dst, send, recv, k, j):
        return pltpu.make_async_remote_copy(
            src_ref=src, dst_ref=dst, send_sem=send, recv_sem=recv,
            device_id=(tm(k), rw(j)), device_id_type=pl.DeviceIdType.MESH,
        )

    loads = [
        pltpu.make_async_copy(video.at[f], raw.at[2 + f, pl.ds(1, BAND)], load_sem.at[f])
        for f in range(FRAMES)
    ]
    loads.append(pltpu.make_async_copy(cw_hbm, cw, load_sem.at[FRAMES]))
    loads.append(pltpu.make_async_copy(dw_hbm, dw, load_sem.at[FRAMES + 1]))
    small = [(clip_hbm, clip), (gain_hbm, gain), (shift_hbm, shift), (cbias_hbm, cbias), (dbias_hbm, dbias)]
    for n, (source, target) in enumerate(small):
        loads.append(pltpu.make_async_copy(source, target, load_sem.at[FRAMES + 2 + n]))
    for copy in loads:
        copy.start()

    barrier = pltpu.get_barrier_semaphore()
    peers = [(0, j) for j in range(1, ROWS)] + [(k, 0) for k in (-2, -1, 1, 2)]
    peers += [(1, 1), (1, -1), (-1, 1), (-1, -1)]
    for k, j in peers:
        pl.semaphore_signal(
            barrier, inc=1, device_id=(tm(k), rw(j)), device_id_type=pl.DeviceIdType.MESH
        )

    for f in range(FRAMES):
        loads[f].wait()

        def add_row(i, sums, f=f):
            x = raw[2 + f, 1 + i].astype(F32).reshape(COLS // 8, 8, CH)
            return sums[0] + jnp.sum(x, axis=0), sums[1] + jnp.sum(x * x, axis=0)

        zero = jnp.zeros((8, CH), F32)
        s, q = lax.fori_loop(0, BAND, add_row, (zero, zero))
        part[pl.ds(f, 1)] = jnp.sum(s, axis=0, keepdims=True)
        part[pl.ds(FRAMES + f, 1)] = jnp.sum(q, axis=0, keepdims=True)

    pl.semaphore_wait(barrier, len(peers))

    tbuf[2] = part[...]
    tcopies = [
        remote(part, tbuf.at[2 - k], t_send.at[2 - k], t_recv.at[2 - k], k, 0)
        for k in (1, 2, -1, -2)
    ]
    for copy in tcopies:
        copy.start()
    halos = [
        remote(video.at[pl.ds(2, 2), pl.ds(4, 4)], raw.at[pl.ds(0, 2), pl.ds(5, 4)], halo_send.at[0], halo_recv.at[0], 1, 0),
        remote(video.at[:, BAND - 1], raw.at[pl.ds(2, FRAMES), 0], halo_send.at[1], halo_recv.at[1], 0, 1),
        remote(video.at[pl.ds(0, 2), 0], raw.at[pl.ds(2, 2), BAND + 1], halo_send.at[2], halo_recv.at[2], 0, -1),
        remote(video.at[pl.ds(2, 2), BAND - 1], raw.at[pl.ds(0, 2), 0], halo_send.at[3], halo_recv.at[3], 1, 1),
        remote(video.at[pl.ds(2, 2), 0], raw.at[pl.ds(0, 2), BAND + 1], halo_send.at[4], halo_recv.at[4], 1, -1),
        remote(video.at[pl.ds(2, 2), pl.ds(0, 4)], raw.at[pl.ds(0, 2), pl.ds(1, 4)], halo_send.at[5], halo_recv.at[5], 1, 0),
        remote(video.at[pl.ds(2, 2), 0], raw.at[pl.ds(4, 2), BAND + 1], halo_send.at[6], halo_recv.at[6], 0, -1),
    ]
    halos[2].start()
    halos[0].start()

    for copy in loads[FRAMES + 2:]:
        copy.wait()

    base = d * FRAMES - 2
    firsts, ends = [], []
    for e in range(EXT + 1):
        first, end, start = jnp.int32(0), jnp.int32(0), jnp.int32(0)
        for c in range(8):
            stop = start + clip[c]
            inside = (base + e >= start) & (base + e < stop)
            first = jnp.where(inside, start, first)
            end = jnp.where(inside, stop, end)
            start = stop
        firsts.append(first - base)
        ends.append(end - base)
    sub = lax.broadcasted_iota(jnp.int32, (8, CH), 0)
    count = jnp.ones((8, CH), F32)
    for e in range(EXT):
        frames = jnp.maximum(ends[e] - firsts[e], 1)
        count = jnp.where(sub == e, (frames * (HEIGHT * COLS * PER_GROUP)).astype(F32), count)

    for copy in tcopies:
        copy.wait_recv()
    mom[...] = jnp.zeros((16, CH), F32)
    for e in range(EXT):
        mine = jnp.zeros((8, CH), F32)
        for k in range(5):
            at = lax.rem(sub, FRAMES) + (2 + (k - 2) * FRAMES)
            mine = mine + jnp.where((at >= firsts[e]) & (at < ends[e]), tbuf[k], 0.0)
        mom[pl.ds(e, 1)] = jnp.sum(jnp.where(sub < FRAMES, mine, 0.0), axis=0, keepdims=True)
        mom[pl.ds(8 + e, 1)] = jnp.sum(jnp.where(sub >= FRAMES, mine, 0.0), axis=0, keepdims=True)
    rcopies = [
        remote(mom, rbuf.at[j], r_send.at[j], r_recv.at[j], 0, j) for j in range(1, ROWS)
    ]
    for copy in rcopies:
        copy.start()
    for j in (6, 1, 4, 5, 3):
        halos[j].start()

    loads[FRAMES].wait()
    loads[FRAMES + 1].wait()

    def lay_conv(a, carry):
        for rr in range(4):
            for e in range(3):
                at = pl.ds((rr * 3 + e) * CH, CH)
                empty = jnp.zeros((CH, CH), BF16)
                wc[a, at, pl.ds(0, CH)] = cw[a, rr, e] if rr < 3 else empty
                wc[a, at, pl.ds(CH, CH)] = cw[a, rr - 1, e] if rr > 0 else empty
        return carry

    lax.fori_loop(0, 3, lay_conv, 0)
    for a in range(3):
        for be in range(9):
            wd[pl.ds(be * CH, CH), pl.ds(a * CH, CH)] = dw[a, be // 3, be % 3]
    lane_a = lax.broadcasted_iota(jnp.int32, (CH, CH), 0) // PER_GROUP
    lane_b = lax.broadcasted_iota(jnp.int32, (CH, CH), 1) // PER_GROUP
    same = jnp.where(lane_a == lane_b, 1.0, 0.0).astype(F32)

    for copy in rcopies:
        copy.wait_recv()
    total = mom[...]
    for j in range(1, ROWS):
        total = total + rbuf[j]
    grouped = jnp.dot(total, same, preferred_element_type=F32, precision=lax.Precision.HIGHEST)
    mean = grouped[0:8] / count
    scale = lax.rsqrt(grouped[8:16] / count - mean * mean + EPSILON)
    slope = scale * gain[...]
    coef[0] = 0.5 * slope
    coef[1] = 0.5 * (shift[...] - mean * slope)

    def activate(frames, group):
        for f in frames:
            for q in range(2):
                i = 2 * group + q
                pick = i
                if i == 0:
                    pick = jnp.where(r == 0, 1, 0)
                if i == BAND + 1:
                    pick = jnp.where(r == ROWS - 1, BAND, BAND + 1)
                x = raw[f, pick].astype(F32)
                h = x * coef[0, pl.ds(f, 1)] + coef[1, pl.ds(f, 1)]
                v = h * jnp.tanh(h) + h
                slot = 2 * (f % 2) + q
                hs[slot, pl.ds(8, COLS)] = v
                hs[slot, pl.ds(7, 1)] = v[0:1]
                hs[slot, pl.ds(8 + COLS, 1)] = v[COLS - 1:COLS]
                hid[group][f, q, :, pl.ds(0, CH)] = hs[slot, pl.ds(7, COLS)].astype(BF16)
                hid[group][f, q, :, pl.ds(CH, CH)] = v.astype(BF16)
                hid[group][f, q, :, pl.ds(2 * CH, CH)] = hs[slot, pl.ds(9, COLS)].astype(BF16)

    def spread(y, f, row, slot):
        ss[slot, pl.ds(8, COLS)] = y
        ss[slot, pl.ds(7, 1)] = y[0:1]
        for e in range(3):
            dn[f, row, :, pl.ds(e * CH, CH)] = ss[slot, pl.ds(7 + e, OUT_COLS, stride=2)].astype(BF16)

    rowcopies = [
        remote(rowsend.at[pl.ds(2, 2)], rowrecv.at[pl.ds(2, 2)], row_send.at[0], row_recv.at[0], 0, 1),
        remote(rowsend.at[pl.ds(0, 2)], rowrecv.at[pl.ds(0, 2)], row_send.at[1], row_recv.at[1], 0, 1),
    ]

    def convolve(f, p):
        acc = None
        for a in range(3):
            at = jnp.maximum(f - 2 + a, firsts[f])
            taps = jnp.concatenate(
                [hid[p][at, 0], hid[p][at, 1], hid[p + 1][at, 0], hid[p + 1][at, 1]], axis=-1
            )
            term = jnp.dot(taps, wc[a], preferred_element_type=F32)
            acc = term if acc is None else acc + term
        for half in range(2):
            y = acc[:, half * CH:(half + 1) * CH] + cbias[...]
            y = y + raw[f, 2 * p + 1 + half].astype(F32)
            spread(y, f - 2, 2 * p + 1 + half, half)
            if p == BAND // 2 - 1 and half == 1:
                rowsend[f - 2] = y.astype(BF16)

    def upper(pair):
        for f in pair:
            spread(rowrecv[f - 2].astype(F32), f - 2, 0, 0)

            @pl.when(r == 0)
            def _(f=f):
                dn[f - 2, 0] = dn[f - 2, 1]

    def downsample(frames, rows):
        taps = jnp.concatenate(
            [
                jnp.concatenate([dn[s, 2 * i + b] for b in range(3)], axis=-1)
                for s in frames
                for i in rows
            ],
            axis=0,
        )
        res = jnp.dot(taps, wd[...], preferred_element_type=F32)
        n = len(rows) * OUT_COLS
        for k, s in enumerate(frames):
            z[s, pl.ds(rows[0] * OUT_COLS, n)] = res[k * n:(k + 1) * n]

    def partial_sums(start, n):
        at = pl.ds(start, n)
        psend[0, at] = z[3, at, lane[1]] + z[ahead, at, lane[0]]
        psend[1, at] = z[3, at, lane[0]]

    lane = [pl.ds(a * CH, CH) for a in range(3)]

    ahead = jnp.minimum(jnp.maximum(firsts[EXT] - 2, 2), 3)
    own, late, early, before = (2, 3, 4, 5), (4, 5), (2, 3), (0, 1)
    top, rest = pl.ds(0, OUT_COLS), pl.ds(OUT_COLS, 3 * OUT_COLS)
    pcopies = [
        remote(psend.at[:, rest], precv.at[:, rest], p_send.at[0], p_recv.at[0], 1, 0),
        remote(psend.at[:, top], precv.at[:, top], p_send.at[1], p_recv.at[1], 1, 0),
    ]

    activate(own, 3)
    activate(own, 2)
    for f in late:
        convolve(f, 2)
    activate(own, 1)
    halos[2].wait_recv()
    halos[6].wait_recv()
    for f in late:
        convolve(f, 1)
    activate(own, 4)
    halos[1].wait_recv()
    for f in late:
        convolve(f, 3)
    activate(own, 0)
    rowcopies[0].start()
    halos[0].wait_recv()
    halos[4].wait_recv()
    for f in late:
        convolve(f, 0)
    activate(before, 4)
    activate(before, 3)
    downsample((2, 3), (1, 2, 3))
    partial_sums(OUT_COLS, 3 * OUT_COLS)
    pcopies[0].start()

    for f in early:
        convolve(f, 3)
    halos[5].wait_recv()
    activate(before, 2)
    rowcopies[1].start()
    for f in early:
        convolve(f, 2)
    activate(before, 1)
    rowcopies[0].wait_recv()
    upper(late)
    downsample((2, 3), (0,))
    partial_sums(0, OUT_COLS)
    pcopies[1].start()
    for f in early:
        convolve(f, 1)
    halos[3].wait_recv()
    activate(before, 0)
    for f in early:
        convolve(f, 0)
    downsample((0, 1), (1, 2, 3))
    rowcopies[1].wait_recv()
    upper(early)
    downsample((0, 1), (0,))
    for copy in pcopies:
        copy.wait_recv()

    for t in range(FRAMES):
        first = firsts[t + 2] - 2
        total = z[t, :, lane[2]] + dbias[...]
        one = jnp.maximum(jnp.maximum(t - 1, first), 0)
        two = jnp.maximum(jnp.maximum(t - 2, first), 0)
        if t == 0:
            rest = jnp.where(first < 0, precv[0], z[0, :, lane[1]] + z[0, :, lane[0]])
        elif t == 1:
            rest = z[one, :, lane[1]] + jnp.where(first < 0, precv[1], z[two, :, lane[0]])
        else:
            rest = z[one, :, lane[1]] + z[two, :, lane[0]]
        out[t] = (total + rest).astype(BF16).reshape(OUT_ROWS, OUT_COLS, CH)

    for copy in halos + rcopies + tcopies + rowcopies + pcopies:
        copy.wait_send()


def per_device(video, clip_lengths, gain, shift, conv_weight, conv_bias, down_weight, down_bias):
    hbm = pl.BlockSpec(memory_space=pltpu.HBM)
    vmem = pl.BlockSpec(memory_space=pltpu.VMEM)
    dma = pltpu.SemaphoreType.DMA
    pixels = OUT_ROWS * OUT_COLS
    return pl.pallas_call(
        kernel,
        out_shape=jax.ShapeDtypeStruct((FRAMES, OUT_ROWS, OUT_COLS, CH), BF16),
        in_specs=[hbm] * 8,
        out_specs=vmem,
        scratch_shapes=[
            pltpu.SMEM((8,), jnp.int32),
            *[pltpu.VMEM((1, CH), F32)] * 4,
            pltpu.VMEM((EXT, BAND + 2, COLS, CH), BF16),
            *[pltpu.VMEM((EXT, 2, COLS, 3 * CH), BF16)] * 5,
            pltpu.VMEM((3, 3, 3, CH, CH), BF16),
            pltpu.VMEM((3, 3, 3, CH, CH), BF16),
            pltpu.VMEM((3, 12 * CH, 2 * CH), BF16),
            pltpu.VMEM((9 * CH, 3 * CH), BF16),
            pltpu.VMEM((8, CH), F32),
            pltpu.VMEM((ROWS, 16, CH), F32),
            pltpu.VMEM((5, 8, CH), F32),
            pltpu.VMEM((16, CH), F32),
            pltpu.VMEM((2, 8, CH), F32),
            pltpu.VMEM((4, COLS + 16, CH), F32),
            pltpu.VMEM((2, COLS + 8, CH), F32),
            pltpu.VMEM((FRAMES, BAND + 1, OUT_COLS, 3 * CH), BF16),
            pltpu.VMEM((FRAMES, COLS, CH), BF16),
            pltpu.VMEM((FRAMES, COLS, CH), BF16),
            pltpu.VMEM((FRAMES, pixels, 3 * CH), F32),
            pltpu.VMEM((2, pixels, CH), F32),
            pltpu.VMEM((2, pixels, CH), F32),
            dma((FRAMES + 7,)),
            dma((7,)), dma((7,)),
            dma((ROWS,)), dma((ROWS,)),
            dma((5,)), dma((5,)),
            dma((2,)), dma((2,)),
            dma((2,)), dma((2,)),
        ],
        compiler_params=pltpu.CompilerParams(
            collective_id=0, has_side_effects=True, vmem_limit_bytes=56 * 1024 * 1024
        ),
        cost_estimate=pl.CostEstimate(
            flops=9_060_000_000, bytes_accessed=5_000_000, transcendentals=2_000_000
        ),
        name="encode",
    )(
        video, clip_lengths, gain.reshape(1, CH), shift.reshape(1, CH),
        conv_weight, conv_bias.reshape(1, CH), down_weight, down_bias.reshape(1, CH),
    )


def solution(mesh):
    placed = (P("tm", "rows", None, None), P(), P(), P(), P(), P(), P(), P())
    return jax.shard_map(
        per_device, mesh=mesh, in_specs=placed,
        out_specs=P("tm", "rows", None, None), check_vma=False,
    )
```

```python
import jax
import jax.numpy as jnp
from jax import lax
from jax.experimental import pallas as pl
from jax.experimental.pallas import tpu as pltpu
from jax.sharding import PartitionSpec as P

GROUPS = 32
EPSILON = 1e-06
TM, ROWS = 8, 16
FRAMES, BAND, COLS, CH = 4, 8, 256, 128
HEIGHT = BAND * ROWS
PER_GROUP = CH // GROUPS
EXT = FRAMES + 2
OUT_ROWS, OUT_COLS = BAND // 2, COLS // 2
F32, BF16 = jnp.float32, jnp.bfloat16


def kernel(
    video, clip_hbm, gain_hbm, shift_hbm, cw_hbm, cbias_hbm, dw_hbm, dbias_hbm, out,
    clip, gain, shift, cbias, dbias, raw, hid0, hid1, hid2, hid3, hid4, cw, dw, wc, wd, part, rbuf, tbuf, mom, coef, hs, ss, dn,
    rowsend, rowrecv, z, psend, precv,
    load_sem, halo_send, halo_recv, r_send, r_recv, t_send, t_recv,
    row_send, row_recv, p_send, p_recv,
):
    hid = (hid0, hid1, hid2, hid3, hid4)
    d = lax.axis_index("tm")
    r = lax.axis_index("rows")

    def tm(k):
        return lax.rem(d + (k + TM), TM)

    def rw(k):
        return lax.rem(r + (k + ROWS), ROWS)

    def remote(src, dst, send, recv, k, j):
        return pltpu.make_async_remote_copy(
            src_ref=src, dst_ref=dst, send_sem=send, recv_sem=recv,
            device_id=(tm(k), rw(j)), device_id_type=pl.DeviceIdType.MESH,
        )

    loads = [
        pltpu.make_async_copy(video.at[f], raw.at[2 + f, pl.ds(1, BAND)], load_sem.at[f])
        for f in range(FRAMES)
    ]
    loads.append(pltpu.make_async_copy(cw_hbm, cw, load_sem.at[FRAMES]))
    loads.append(pltpu.make_async_copy(dw_hbm, dw, load_sem.at[FRAMES + 1]))
    small = [(clip_hbm, clip), (gain_hbm, gain), (shift_hbm, shift), (cbias_hbm, cbias), (dbias_hbm, dbias)]
    for n, (source, target) in enumerate(small):
        loads.append(pltpu.make_async_copy(source, target, load_sem.at[FRAMES + 2 + n]))
    for copy in loads[:FRAMES] + loads[FRAMES + 2:]:
        copy.start()

    barrier = pltpu.get_barrier_semaphore()
    peers = [(0, j) for j in range(1, ROWS)] + [(k, 0) for k in (-2, -1, 1, 2)]
    peers += [(1, 1), (1, -1), (-1, 1), (-1, -1)]
    for k, j in peers:
        pl.semaphore_signal(
            barrier, inc=1, device_id=(tm(k), rw(j)), device_id_type=pl.DeviceIdType.MESH
        )

    for f in range(FRAMES):
        loads[f].wait()

        def add_row(i, sums, f=f):
            x = raw[2 + f, 1 + i].astype(F32).reshape(COLS // 8, 8, CH)
            return sums[0] + jnp.sum(x, axis=0), sums[1] + jnp.sum(x * x, axis=0)

        zero = jnp.zeros((8, CH), F32)
        s, q = lax.fori_loop(0, BAND, add_row, (zero, zero))
        part[pl.ds(f, 1)] = jnp.sum(s, axis=0, keepdims=True)
        part[pl.ds(FRAMES + f, 1)] = jnp.sum(q, axis=0, keepdims=True)

    for copy in loads[FRAMES:FRAMES + 2]:
        copy.start()
    pl.semaphore_wait(barrier, len(peers))

    tbuf[2] = part[...]
    tcopies = [
        remote(part, tbuf.at[2 - k], t_send.at[2 - k], t_recv.at[2 - k], k, 0)
        for k in (1, 2, -1, -2)
    ]
    for copy in tcopies:
        copy.start()
    halos = [
        remote(video.at[pl.ds(2, 2), pl.ds(4, 4)], raw.at[pl.ds(0, 2), pl.ds(5, 4)], halo_send.at[0], halo_recv.at[0], 1, 0),
        remote(video.at[:, BAND - 1], raw.at[pl.ds(2, FRAMES), 0], halo_send.at[1], halo_recv.at[1], 0, 1),
        remote(video.at[pl.ds(0, 2), 0], raw.at[pl.ds(2, 2), BAND + 1], halo_send.at[2], halo_recv.at[2], 0, -1),
        remote(video.at[pl.ds(2, 2), BAND - 1], raw.at[pl.ds(0, 2), 0], halo_send.at[3], halo_recv.at[3], 1, 1),
        remote(video.at[pl.ds(2, 2), 0], raw.at[pl.ds(0, 2), BAND + 1], halo_send.at[4], halo_recv.at[4], 1, -1),
        remote(video.at[pl.ds(2, 2), pl.ds(0, 4)], raw.at[pl.ds(0, 2), pl.ds(1, 4)], halo_send.at[5], halo_recv.at[5], 1, 0),
        remote(video.at[pl.ds(2, 2), 0], raw.at[pl.ds(4, 2), BAND + 1], halo_send.at[6], halo_recv.at[6], 0, -1),
    ]
    halos[2].start()
    halos[0].start()

    for copy in loads[FRAMES + 2:]:
        copy.wait()

    base = d * FRAMES - 2
    firsts, ends = [], []
    for e in range(EXT + 1):
        first, end, start = jnp.int32(0), jnp.int32(0), jnp.int32(0)
        for c in range(8):
            stop = start + clip[c]
            inside = (base + e >= start) & (base + e < stop)
            first = jnp.where(inside, start, first)
            end = jnp.where(inside, stop, end)
            start = stop
        firsts.append(first - base)
        ends.append(end - base)
    sub = lax.broadcasted_iota(jnp.int32, (8, CH), 0)
    count = jnp.ones((8, CH), F32)
    for e in range(EXT):
        frames = jnp.maximum(ends[e] - firsts[e], 1)
        count = jnp.where(sub == e, (frames * (HEIGHT * COLS * PER_GROUP)).astype(F32), count)

    for copy in tcopies:
        copy.wait_recv()
    mom[...] = jnp.zeros((16, CH), F32)
    for e in range(EXT):
        mine = jnp.zeros((8, CH), F32)
        for k in range(5):
            at = lax.rem(sub, FRAMES) + (2 + (k - 2) * FRAMES)
            mine = mine + jnp.where((at >= firsts[e]) & (at < ends[e]), tbuf[k], 0.0)
        mom[pl.ds(e, 1)] = jnp.sum(jnp.where(sub < FRAMES, mine, 0.0), axis=0, keepdims=True)
        mom[pl.ds(8 + e, 1)] = jnp.sum(jnp.where(sub >= FRAMES, mine, 0.0), axis=0, keepdims=True)
    rcopies = [
        remote(mom, rbuf.at[j], r_send.at[j], r_recv.at[j], 0, j) for j in range(1, ROWS)
    ]
    for copy in rcopies:
        copy.start()
    for j in (6, 1, 4, 5, 3):
        halos[j].start()

    loads[FRAMES].wait()
    loads[FRAMES + 1].wait()

    def lay_conv(a, carry):
        for rr in range(4):
            for e in range(3):
                at = pl.ds((rr * 3 + e) * CH, CH)
                empty = jnp.zeros((CH, CH), BF16)
                wc[a, at, pl.ds(0, CH)] = cw[a, rr, e] if rr < 3 else empty
                wc[a, at, pl.ds(CH, CH)] = cw[a, rr - 1, e] if rr > 0 else empty
        return carry

    lax.fori_loop(0, 3, lay_conv, 0)
    for a in range(3):
        for be in range(9):
            wd[pl.ds(be * CH, CH), pl.ds(a * CH, CH)] = dw[a, be // 3, be % 3]
    lane_a = lax.broadcasted_iota(jnp.int32, (CH, CH), 0) // PER_GROUP
    lane_b = lax.broadcasted_iota(jnp.int32, (CH, CH), 1) // PER_GROUP
    same = jnp.where(lane_a == lane_b, 1.0, 0.0).astype(F32)

    for copy in rcopies:
        copy.wait_recv()
    total = mom[...]
    for j in range(1, ROWS):
        total = total + rbuf[j]
    grouped = jnp.dot(total, same, preferred_element_type=F32, precision=lax.Precision.HIGHEST)
    mean = grouped[0:8] / count
    scale = lax.rsqrt(grouped[8:16] / count - mean * mean + EPSILON)
    slope = scale * gain[...]
    coef[0] = 0.5 * slope
    coef[1] = 0.5 * (shift[...] - mean * slope)

    def activate(frames, group):
        for f in frames:
            for q in range(2):
                i = 2 * group + q
                pick = i
                if i == 0:
                    pick = jnp.where(r == 0, 1, 0)
                if i == BAND + 1:
                    pick = jnp.where(r == ROWS - 1, BAND, BAND + 1)
                x = raw[f, pick].astype(F32)
                h = x * coef[0, pl.ds(f, 1)] + coef[1, pl.ds(f, 1)]
                v = h * jnp.tanh(h) + h
                slot = 2 * (f % 2) + q
                hs[slot, pl.ds(8, COLS)] = v
                hs[slot, pl.ds(7, 1)] = v[0:1]
                hs[slot, pl.ds(8 + COLS, 1)] = v[COLS - 1:COLS]
                hid[group][f, q, :, pl.ds(0, CH)] = hs[slot, pl.ds(7, COLS)].astype(BF16)
                hid[group][f, q, :, pl.ds(CH, CH)] = v.astype(BF16)
                hid[group][f, q, :, pl.ds(2 * CH, CH)] = hs[slot, pl.ds(9, COLS)].astype(BF16)

    def spread(y, f, row, slot):
        ss[slot, pl.ds(8, COLS)] = y
        ss[slot, pl.ds(7, 1)] = y[0:1]
        for e in range(3):
            dn[f, row, :, pl.ds(e * CH, CH)] = ss[slot, pl.ds(7 + e, OUT_COLS, stride=2)].astype(BF16)

    rowcopies = [
        remote(rowsend.at[pl.ds(2, 2)], rowrecv.at[pl.ds(2, 2)], row_send.at[0], row_recv.at[0], 0, 1),
        remote(rowsend.at[pl.ds(0, 2)], rowrecv.at[pl.ds(0, 2)], row_send.at[1], row_recv.at[1], 0, 1),
    ]

    def convolve(f, p):
        acc = None
        for a in range(3):
            at = jnp.maximum(f - 2 + a, firsts[f])
            taps = jnp.concatenate(
                [hid[p][at, 0], hid[p][at, 1], hid[p + 1][at, 0], hid[p + 1][at, 1]], axis=-1
            )
            term = jnp.dot(taps, wc[a], preferred_element_type=F32)
            acc = term if acc is None else acc + term
        for half in range(2):
            y = acc[:, half * CH:(half + 1) * CH] + cbias[...]
            y = y + raw[f, 2 * p + 1 + half].astype(F32)
            spread(y, f - 2, 2 * p + 1 + half, half)
            if p == BAND // 2 - 1 and half == 1:
                rowsend[f - 2] = y.astype(BF16)

    def upper(pair):
        for f in pair:
            spread(rowrecv[f - 2].astype(F32), f - 2, 0, 0)

            @pl.when(r == 0)
            def _(f=f):
                dn[f - 2, 0] = dn[f - 2, 1]

    def downsample(frames, rows):
        taps = jnp.concatenate(
            [
                jnp.concatenate([dn[s, 2 * i + b] for b in range(3)], axis=-1)
                for s in frames
                for i in rows
            ],
            axis=0,
        )
        res = jnp.dot(taps, wd[...], preferred_element_type=F32)
        n = len(rows) * OUT_COLS
        for k, s in enumerate(frames):
            z[s, pl.ds(rows[0] * OUT_COLS, n)] = res[k * n:(k + 1) * n]

    def partial_sums(start, n):
        at = pl.ds(start, n)
        psend[0, at] = z[3, at, lane[1]] + z[ahead, at, lane[0]]
        psend[1, at] = z[3, at, lane[0]]

    lane = [pl.ds(a * CH, CH) for a in range(3)]

    ahead = jnp.minimum(jnp.maximum(firsts[EXT] - 2, 2), 3)
    own, late, early, before = (2, 3, 4, 5), (4, 5), (2, 3), (0, 1)
    top, rest = pl.ds(0, OUT_COLS), pl.ds(OUT_COLS, 3 * OUT_COLS)
    pcopies = [
        remote(psend.at[:, rest], precv.at[:, rest], p_send.at[0], p_recv.at[0], 1, 0),
        remote(psend.at[:, top], precv.at[:, top], p_send.at[1], p_recv.at[1], 1, 0),
    ]

    activate(own, 3)
    activate(own, 2)
    for f in late:
        convolve(f, 2)
    activate(own, 1)
    halos[2].wait_recv()
    halos[6].wait_recv()
    for f in late:
        convolve(f, 1)
    activate(own, 4)
    halos[1].wait_recv()
    for f in late:
        convolve(f, 3)
    activate(own, 0)
    rowcopies[0].start()
    halos[0].wait_recv()
    halos[4].wait_recv()
    for f in late:
        convolve(f, 0)
    activate(before, 4)
    activate(before, 3)
    downsample((2, 3), (1, 2, 3))
    partial_sums(OUT_COLS, 3 * OUT_COLS)
    pcopies[0].start()

    for f in early:
        convolve(f, 3)
    halos[5].wait_recv()
    activate(before, 2)
    rowcopies[1].start()
    for f in early:
        convolve(f, 2)
    activate(before, 1)
    rowcopies[0].wait_recv()
    upper(late)
    downsample((2, 3), (0,))
    partial_sums(0, OUT_COLS)
    pcopies[1].start()
    for f in early:
        convolve(f, 1)
    halos[3].wait_recv()
    activate(before, 0)
    for f in early:
        convolve(f, 0)
    downsample((0, 1), (1, 2, 3))
    rowcopies[1].wait_recv()
    upper(early)
    downsample((0, 1), (0,))
    for copy in pcopies:
        copy.wait_recv()

    for t in range(FRAMES):
        first = firsts[t + 2] - 2
        total = z[t, :, lane[2]] + dbias[...]
        one = jnp.maximum(jnp.maximum(t - 1, first), 0)
        two = jnp.maximum(jnp.maximum(t - 2, first), 0)
        if t == 0:
            rest = jnp.where(first < 0, precv[0], z[0, :, lane[1]] + z[0, :, lane[0]])
        elif t == 1:
            rest = z[one, :, lane[1]] + jnp.where(first < 0, precv[1], z[two, :, lane[0]])
        else:
            rest = z[one, :, lane[1]] + z[two, :, lane[0]]
        out[t] = (total + rest).astype(BF16).reshape(OUT_ROWS, OUT_COLS, CH)

    for copy in halos + rcopies + tcopies + rowcopies + pcopies:
        copy.wait_send()


def per_device(video, clip_lengths, gain, shift, conv_weight, conv_bias, down_weight, down_bias):
    hbm = pl.BlockSpec(memory_space=pltpu.HBM)
    vmem = pl.BlockSpec(memory_space=pltpu.VMEM)
    dma = pltpu.SemaphoreType.DMA
    pixels = OUT_ROWS * OUT_COLS
    return pl.pallas_call(
        kernel,
        out_shape=jax.ShapeDtypeStruct((FRAMES, OUT_ROWS, OUT_COLS, CH), BF16),
        in_specs=[hbm] * 8,
        out_specs=vmem,
        scratch_shapes=[
            pltpu.SMEM((8,), jnp.int32),
            *[pltpu.VMEM((1, CH), F32)] * 4,
            pltpu.VMEM((EXT, BAND + 2, COLS, CH), BF16),
            *[pltpu.VMEM((EXT, 2, COLS, 3 * CH), BF16)] * 5,
            pltpu.VMEM((3, 3, 3, CH, CH), BF16),
            pltpu.VMEM((3, 3, 3, CH, CH), BF16),
            pltpu.VMEM((3, 12 * CH, 2 * CH), BF16),
            pltpu.VMEM((9 * CH, 3 * CH), BF16),
            pltpu.VMEM((8, CH), F32),
            pltpu.VMEM((ROWS, 16, CH), F32),
            pltpu.VMEM((5, 8, CH), F32),
            pltpu.VMEM((16, CH), F32),
            pltpu.VMEM((2, 8, CH), F32),
            pltpu.VMEM((4, COLS + 16, CH), F32),
            pltpu.VMEM((2, COLS + 8, CH), F32),
            pltpu.VMEM((FRAMES, BAND + 1, OUT_COLS, 3 * CH), BF16),
            pltpu.VMEM((FRAMES, COLS, CH), BF16),
            pltpu.VMEM((FRAMES, COLS, CH), BF16),
            pltpu.VMEM((FRAMES, pixels, 3 * CH), F32),
            pltpu.VMEM((2, pixels, CH), F32),
            pltpu.VMEM((2, pixels, CH), F32),
            dma((FRAMES + 7,)),
            dma((7,)), dma((7,)),
            dma((ROWS,)), dma((ROWS,)),
            dma((5,)), dma((5,)),
            dma((2,)), dma((2,)),
            dma((2,)), dma((2,)),
        ],
        compiler_params=pltpu.CompilerParams(
            collective_id=0, has_side_effects=True, vmem_limit_bytes=56 * 1024 * 1024
        ),
        cost_estimate=pl.CostEstimate(
            flops=9_060_000_000, bytes_accessed=5_000_000, transcendentals=2_000_000
        ),
        name="encode",
    )(
        video, clip_lengths, gain.reshape(1, CH), shift.reshape(1, CH),
        conv_weight, conv_bias.reshape(1, CH), down_weight, down_bias.reshape(1, CH),
    )


def solution(mesh):
    placed = (P("tm", "rows", None, None), P(), P(), P(), P(), P(), P(), P())
    return jax.shard_map(
        per_device, mesh=mesh, in_specs=placed,
        out_specs=P("tm", "rows", None, None), check_vma=False,
    )
```
